256 devices in a mesh: freq: 8 (over y, core), site: 32 (over z, x).
Axes of the slice: x: 4, y: 4, z: 8, core: 2. Of those that a mesh axis runs over, the one named last changes fastest.
Arguments:
- incident: float32 [512, 32, 2, 512], P('site', 'freq'), parts along dimension 1, may hold values from -6 to 6
- diffraction: float32 [16, 512, 512], P('freq'), parts along dimension 0, may hold values from -0.1875 to 0.1875
- mixing: float32 [16, 512, 512], P('freq'), parts along dimension 0, may hold values from -0.1875 to 0.1875
- coupling: float32 [512, 64, 2, 512], P('site', 'freq'), parts along dimension 1, may hold values from -1.2 to 1.2
- lists: int32 [512, 8], P('site'), may hold values from 0 to 511, as said below
- groups: int32 [512, 1], P('site'), may hold values from 0 to 31; in each aligned block of 16 rows (0 to 15, 16 to 31, ...) at most 4 rows name the same one
- jacket: float32 [32, 16, 512, 128], P('site', 'freq'), parts along dimension 1, may hold values from -0.046875 to 0.046875
Outputs:
- coefficients: float32 [512, 32, 2, 512], P('site', 'freq'), parts along dimension 1
- response: float32 [32, 32, 2, 128], P('site', 'freq'), parts along dimension 1
The draws below stay inside these ranges and needn't reach their ends.
There are 8 independent parts, one for each index of `freq`. The reference program is written for one: setup_inputs(seed, part) draws one part's arguments, and reference() takes and returns one part's arrays. A program takes and returns all parts, laid end to end along the dimension named above; an argument that names none is the same for every part. Nothing has to cross between parts.
Inputs may be any that keep to these rules, and one draw needn't show every extreme that they name: No list names its own body or repeats a body; each body lists exactly 4 other bodies of its own index of site and 4 bodies of other indices; the lists of one index's bodies name exactly 2 distinct bodies of every other index of site. `groups`: among the bodies of one index of site at most 4 belong to the same group.
All inputs are finite; a program needn't handle non-finite values.
Results may differ from the reference program's by a relative error of at most 0.00012.
Values sent between devices are 32-bit elements; how exact they have to be, the bound alone decides.
A program may use at most 64 MiB of HBM per device.

```python
import math
import jax
import jax.numpy as jnp
import numpy as np
from jax import lax

M = 512
NF = 128
HEAD = 4
BDEV = 16
KL = 4
KR = 4
CAP = 2
CAPF = 4
ITERS = 3
K = 8
BODIES = 512
GROUPS = 32


def draw_lists(key, part):
    site_count = BODIES // BDEV
    base_key = jax.random.fold_in(key, 7)
    key_pick, key_pool, key_local, key_order = jax.random.split(base_key, 4)
    pick_keys = jax.random.split(key_pick, site_count * site_count)
    chosen = jax.vmap(lambda entry: jax.random.permutation(entry, BDEV))(pick_keys)
    chosen = chosen.reshape(site_count, site_count, BDEV)[:, :, :CAP].astype(jnp.int32)
    owners = jnp.arange(site_count, dtype=jnp.int32)
    candidates = owners[None, :, None] * BDEV + chosen
    offsets = jnp.arange(site_count - 1, dtype=jnp.int32)
    peers = (owners[:, None] + 1 + offsets[None, :]) % site_count
    pool_size = (site_count - 1) * CAP
    remote_pool = jnp.take_along_axis(candidates, peers[:, :, None], axis=1).reshape(site_count, pool_size)
    pool_keys = jax.random.split(key_pool, site_count)
    shuffles = jax.vmap(lambda entry: jax.random.permutation(entry, pool_size))(pool_keys).astype(jnp.int32)
    remote_pool = jnp.take_along_axis(remote_pool, shuffles, axis=1)
    bodies_local = jnp.arange(BDEV, dtype=jnp.int32)
    spots = (bodies_local[:, None] * KR + jnp.arange(KR, dtype=jnp.int32)[None, :]) % pool_size
    remote = remote_pool[:, spots]
    local_keys = jax.random.split(key_local, site_count * BDEV)
    steps_local = jax.vmap(lambda entry: jax.random.permutation(entry, BDEV - 1))(local_keys)[:, :KL]
    steps_local = steps_local.reshape(site_count, BDEV, KL).astype(jnp.int32) + 1
    near = owners[:, None, None] * BDEV + (bodies_local[None, :, None] + steps_local) % BDEV
    joined = jnp.concatenate([near, remote], axis=2)
    order_keys = jax.random.split(key_order, site_count * BDEV)
    arrange = jax.vmap(lambda entry: jax.random.permutation(entry, K))(order_keys).reshape(site_count, BDEV, K).astype(jnp.int32)
    joined = jnp.take_along_axis(joined, arrange, axis=2)
    return joined.reshape(BODIES, K).astype(jnp.int32)


def shard_levels(stream_key, shape, pieces, smallest, high):
    def one(dim, parts):
        draws = jax.random.uniform(jax.random.fold_in(jax.random.fold_in(stream_key, 6), dim), (parts,), jnp.float32, smallest / len(pieces), high / len(pieces))
        return jnp.repeat(jnp.exp(draws), shape[dim] // parts).reshape((-1,) + (1,) * (len(shape) - dim - 1))

    factor_of = one(*pieces[0])
    for cut in pieces[1:]:
        factor_of = factor_of * one(*cut)
    return factor_of


def deal_out(stream_key, own, number, rows, amount, top, reach, skew):
    sequence = jax.random.permutation(stream_key, amount)
    heavy_load, common = load_shares(amount, rows * top, reach, skew, True), load_shares(amount, rows * top, reach, skew, False)
    places = jnp.arange(amount)

    def named(sizes, turn):
        used = int((sizes > 0).sum())
        fixed = max(1, used // 4)
        passed = fixed + (places - fixed + turn * (used - fixed)) % max(1, amount - fixed)
        return jnp.zeros((amount,), jnp.int32).at[sequence[jnp.where(places < fixed, places, passed)]].set(jnp.asarray(sizes, jnp.int32))

    sizes = jnp.where(number % 4 == 0, named(heavy_load, number // 4), named(common, number - number // 4 - 1))
    mixed = jax.random.permutation(jax.random.fold_in(own, 3), amount)
    source_of, receiver = mixed[0:amount // 2 * 2:2], mixed[1:amount // 2 * 2:2]
    slack = jnp.minimum(sizes[source_of] - 1, reach - sizes[receiver]) // 2
    slack = jnp.where((source_of == sequence[0]) | (receiver == sequence[0]) | (sizes[receiver] == 0), 0, jnp.maximum(slack, 0))
    passed = jax.random.randint(jax.random.fold_in(own, 4), (amount // 2,), 0, 1 << 20) % (slack + 1)
    sizes = sizes.at[source_of].add(-passed).at[receiver].add(passed)
    labels = jnp.searchsorted(jnp.cumsum(sizes), jnp.arange(rows * top), side="right").astype(jnp.int32)
    listing = labels.reshape(top, rows).T
    listing = listing[jax.random.permutation(jax.random.fold_in(own, 1), rows)]
    turn = jax.random.randint(jax.random.fold_in(own, 2), (rows, 1), 0, top)
    return jnp.take_along_axis(listing, (jnp.arange(top)[None, :] + turn) % top, axis=1)


def load_shares(amount, total, most, skew, full):
    loads = [(1 << 20) // math.isqrt(standing ** skew) + 1 for standing in range(1, amount + 1)]
    largest = most if full else min(most, max(-(-total // amount), total * loads[0] // sum(loads)))
    least = 1 if total - largest >= amount - 1 else 0
    holding, rest = [largest] + [least] * (amount - 1), total - largest - least * (amount - 1)
    while rest > 0:
        movable = [i for i in range(1, amount) if holding[i] < largest] or [i for i in range(1, amount) if holding[i] < most]
        whole, budget = sum([loads[i] for i in movable]), rest
        for i in movable:
            extra = min(most - holding[i], max(1, budget * loads[i] // whole), rest)
            holding[i] = holding[i] + extra
            rest = rest - extra
    return np.array(holding)


def centred(key, extent, spread, bound, shards=(), kind=jnp.bfloat16):
    result = jax.random.normal(key, extent, jnp.float32) * spread
    if len(shards) > 0:
        result = shard_levels(key, extent, shards, -0.22, 0.18) * result
    return jnp.clip(result, min=-bound, max=bound).astype(kind)


def setup_inputs(seed: int = 0, part: int = 0) -> dict:
    key_list = jax.random.split(jax.random.key(seed), 8)
    part_keys = jax.random.split(jax.random.fold_in(key_list[7], part), 8)
    incident = centred(part_keys[0], (BODIES, HEAD, 2, M), 1.0, 6.0, ((0, 32),), jnp.float32)
    diffraction = centred(part_keys[1], (2, M, M), (2 * M) ** -0.5, 0.1875, (), jnp.float32)
    mixing = centred(part_keys[2], (2, M, M), (2 * M) ** -0.5, 0.1875, (), jnp.float32)
    coupling = centred(part_keys[3], (BODIES, K, 2, M), 0.2, 1.2, ((0, 32),), jnp.float32)
    lists = draw_lists(jax.random.fold_in(key_list[7], 71), part)
    groups_keys = jax.random.split(jax.random.fold_in(key_list[5], 1), BODIES // BDEV)
    groups_turns = jax.random.permutation(jax.random.fold_in(key_list[5], 3), BODIES // BDEV)
    groups = jax.vmap(lambda own, number: deal_out(jax.random.fold_in(key_list[5], 2), own, number, BDEV, GROUPS, 1, CAPF, 2))(groups_keys, groups_turns).reshape((BODIES, 1))
    jacket = centred(part_keys[6], (GROUPS, 2, M, NF), (2 * M * BDEV) ** -0.5, 0.046875, ((0, 32),), jnp.float32)
    return {"incident": incident, "diffraction": diffraction, "mixing": mixing, "coupling": coupling, "lists": lists, "groups": groups, "jacket": jacket}


def complex_product(values, real_part, imag_part):
    highest = lax.Precision.HIGHEST
    first = values[..., 0, :]
    second = values[..., 1, :]
    real_out = jnp.matmul(first, real_part, precision=highest) - jnp.matmul(second, imag_part, precision=highest)
    imag_out = jnp.matmul(first, imag_part, precision=highest) + jnp.matmul(second, real_part, precision=highest)
    return jnp.stack([real_out, imag_out], axis=-2)


def phase_apply(phase, values):
    real_out = phase[..., 0, :] * values[..., 0, :] - phase[..., 1, :] * values[..., 1, :]
    imag_out = phase[..., 0, :] * values[..., 1, :] + phase[..., 1, :] * values[..., 0, :]
    return jnp.stack([real_out, imag_out], axis=-2)


def reference(incident, diffraction, mixing, coupling, lists, groups, jacket):
    coefficients = complex_product(incident, diffraction[0], diffraction[1])
    for sweep in range(ITERS):
        outgoing = complex_product(coefficients, mixing[0], mixing[1])
        incoming = incident
        for slot_index in range(K):
            fetched = jnp.take(outgoing, lists[:, slot_index].astype(jnp.int32), axis=0)
            incoming = incoming + phase_apply(coupling[:, slot_index][:, None], fetched)
        coefficients = complex_product(incoming, diffraction[0], diffraction[1])
    group_total = jax.ops.segment_sum(coefficients, groups[:, 0].astype(jnp.int32), num_segments=GROUPS)
    response = complex_product(group_total, jacket[:, 0], jacket[:, 1])
    return (coefficients, response)
```

```python
import jax
import jax.numpy as jnp
from jax import lax
from jax.experimental import pallas as pl
from jax.experimental.pallas import tpu as pltpu
from jax.sharding import PartitionSpec as P

ITERS = 3
NZ = 8
NX = 4
SITES = NZ * NX
BDEV = 16
K = 8
M = 512
NF = 128
ROWS = 8
POOL = 2 * SITES + BDEV
MESH = pl.DeviceIdType.MESH
F32 = jnp.float32
BF16 = jnp.bfloat16


def split(x):
    hi = x.astype(BF16)
    lo = (x - hi.astype(F32)).astype(BF16)
    return hi, lo


def turn(x):
    n = x.shape[0]
    even = lax.broadcasted_iota(jnp.int32, x.shape, 0) % 2 == 0
    return jnp.where(even, -pltpu.roll(x, n - 1, 0), pltpu.roll(x, 1, 0))


def product(x, w_hi, w_lo):
    width = w_hi.shape[1] // 2
    x_hi, x_lo = split(x)
    y = jnp.dot(x_hi, w_hi[...], preferred_element_type=F32)
    y = y + jnp.dot(x_lo, w_hi[...], preferred_element_type=F32)
    y = y + jnp.dot(x_hi, w_lo[...], preferred_element_type=F32)
    return y[:, :width] + turn(y[:, width:])


def load_matrix(src, w_hi, w_lo):
    width = src.shape[2]
    for part in range(2):
        hi, lo = split(src[part])
        w_hi[:, part * width : (part + 1) * width] = hi
        w_lo[:, part * width : (part + 1) * width] = lo


def kernel(
    incident,
    diffraction,
    mixing,
    coupling,
    lists,
    groups,
    jacket,
    coef_out,
    resp_out,
    d_hi,
    d_lo,
    m_hi,
    m_lo,
    j_hi,
    j_lo,
    lists_all,
    picks,
    places,
    picks_s,
    places_s,
    sending,
    own,
    pool_first,
    pool_second,
    pool_third,
    incoming,
    shares,
    totals,
    list_sems,
    row_send,
    row_recv,
    share_sems,
    table_sem,
):
    pools = (pool_first, pool_second, pool_third)
    me = lax.axis_index("site")
    z, x = me // NX, me % NX

    def target(slot):
        dz, dx = (slot // NX) * 5 % NZ, slot % NX
        return ((z + dz) % NZ) * NX + (x + dx) % NX

    def back(slot):
        q, dx = slot // NX, slot % NX
        return ((NZ - q) % NZ) * NX + (NX - dx) % NX

    barrier = pltpu.get_barrier_semaphore()

    @pl.loop(1, SITES)
    def _(slot):
        pl.semaphore_signal(barrier, inc=1, device_id={"site": target(slot)}, device_id_type=MESH)

    load_matrix(diffraction, d_hi, d_lo)
    load_matrix(mixing, m_hi, m_lo)
    pl.semaphore_wait(barrier, SITES - 1)

    @pl.loop(1, SITES)
    def _(slot):
        pltpu.make_async_remote_copy(
            src_ref=lists.at[0],
            dst_ref=lists_all.at[back(slot)],
            send_sem=list_sems.at[0],
            recv_sem=list_sems.at[1],
            device_id={"site": target(slot)},
            device_id_type=MESH,
        ).start()

    own_list = lists[0]
    owner = own_list // BDEV
    local = own_list % BDEV
    sites = lax.broadcasted_iota(jnp.int32, (SITES, BDEV * K), 0)
    named = owner == sites
    last = jnp.max(jnp.where(named, local, -1), axis=1, keepdims=True)
    second = jnp.max(jnp.where(named & (local == last), 1, 0), axis=0, keepdims=True)
    dz = (z - owner // NX + NZ) % NZ
    dx = (x - owner % NX + NX) % NX
    slot_of = (dz * 5 % NZ) * NX + dx
    places[...] = jnp.where(owner == me, 2 * SITES + local, 2 * slot_of + second)
    move_places = pltpu.make_async_copy(places, places_s, table_sem.at[0])
    move_places.start()
    load_matrix(jacket, j_hi, j_lo)

    coef = product(incident[...].reshape(BDEV * ROWS, M), d_hi, d_lo)
    own[...] = product(coef, m_hi, m_lo).reshape(BDEV, ROWS, M)

    pltpu.make_async_copy(lists_all.at[1:], lists_all.at[1:], list_sems.at[1]).wait()
    everyone = lists_all[:, 0, :]
    mine = everyone // BDEV == me
    wanted = everyone % BDEV
    first = jnp.min(jnp.where(mine, wanted, BDEV - 1), axis=1, keepdims=True)
    final = jnp.max(jnp.where(mine, wanted, 0), axis=1, keepdims=True)
    lane = lax.broadcasted_iota(jnp.int32, (SITES, 128), 1)
    picks[...] = jnp.where(lane == 0, first, final)
    move_picks = pltpu.make_async_copy(picks, picks_s, table_sem.at[1])
    move_picks.start()
    move_places.wait()
    move_picks.wait()

    for sweep in range(ITERS):
        pool = pools[sweep]

        @pl.loop(1, SITES)
        def _(slot):
            for row in range(2):
                sending[sweep, 2 * slot + row] = own[picks_s[slot, row]]
            pltpu.make_async_remote_copy(
                src_ref=sending.at[sweep, pl.ds(2 * slot, 2)],
                dst_ref=pool.at[pl.ds(2 * slot, 2)],
                send_sem=row_send.at[sweep],
                recv_sem=row_recv.at[sweep],
                device_id={"site": target(slot)},
                device_id_type=MESH,
            ).start()

        pool[2 * SITES :] = own[...]
        arrived = pool.at[pl.ds(2, 2 * SITES - 2)]
        pltpu.make_async_copy(arrived, arrived, row_recv.at[sweep]).wait()

        @pl.loop(0, BDEV)
        def _(body):
            straight = jnp.zeros((ROWS, M), F32)
            turned = jnp.zeros((ROWS, M), F32)
            for k in range(K):
                value = pool[places_s[0, body * K + k]]
                straight = straight + coupling[body, 2 * k : 2 * k + 1, :] * value
                turned = turned + coupling[body, 2 * k + 1 : 2 * k + 2, :] * value
            incoming[body] = incident[body] + straight + turn(turned)

        coef = product(incoming[...].reshape(BDEV * ROWS, M), d_hi, d_lo)
        if sweep < ITERS - 1:
            own[...] = product(coef, m_hi, m_lo).reshape(BDEV, ROWS, M)
    coef_out[...] = coef.reshape(BDEV, ROWS, M)

    @pl.loop(1, SITES)
    def _(slot):
        share = jnp.zeros((ROWS, M), F32)
        peer = target(slot)
        for body in range(BDEV):
            weight = jnp.where(groups[0, body] == peer, 1.0, 0.0)
            share = share + weight * coef_out[body]
        shares[slot] = share
        pltpu.make_async_remote_copy(
            src_ref=shares.at[slot],
            dst_ref=totals.at[slot],
            send_sem=share_sems.at[0],
            recv_sem=share_sems.at[1],
            device_id={"site": peer},
            device_id_type=MESH,
        ).start()

    total = jnp.zeros((ROWS, M), F32)
    for body in range(BDEV):
        weight = jnp.where(groups[0, body] == me, 1.0, 0.0)
        total = total + weight * coef_out[body]
    pltpu.make_async_copy(totals.at[1:], totals.at[1:], share_sems.at[1]).wait()
    for slot in range(1, SITES):
        total = total + totals[slot]
    resp_out[...] = product(total, j_hi, j_lo)

    pltpu.make_async_copy(lists_all.at[1:], lists_all.at[1:], list_sems.at[0]).wait()
    for sweep in range(ITERS):
        sent = sending.at[sweep, pl.ds(2, 2 * SITES - 2)]
        pltpu.make_async_copy(sent, sent, row_send.at[sweep]).wait()
    pltpu.make_async_copy(shares.at[1:], shares.at[1:], share_sems.at[0]).wait()


def per_device(incident, diffraction, mixing, coupling, lists, groups, jacket):
    vmem = pl.BlockSpec(memory_space=pltpu.VMEM)
    smem = pl.BlockSpec(memory_space=pltpu.SMEM)
    coef, resp = pl.pallas_call(
        kernel,
        out_shape=(
            jax.ShapeDtypeStruct((BDEV, ROWS, M), F32),
            jax.ShapeDtypeStruct((ROWS, NF), F32),
        ),
        in_specs=[vmem] * 5 + [smem, vmem],
        out_specs=(vmem, vmem),
        scratch_shapes=[
            pltpu.VMEM((M, 2 * M), BF16),
            pltpu.VMEM((M, 2 * M), BF16),
            pltpu.VMEM((M, 2 * M), BF16),
            pltpu.VMEM((M, 2 * M), BF16),
            pltpu.VMEM((M, 2 * NF), BF16),
            pltpu.VMEM((M, 2 * NF), BF16),
            pltpu.VMEM((SITES, 1, BDEV * K), jnp.int32),
            pltpu.VMEM((SITES, 128), jnp.int32),
            pltpu.VMEM((1, 128), jnp.int32),
            pltpu.SMEM((SITES, 128), jnp.int32),
            pltpu.SMEM((1, 128), jnp.int32),
            pltpu.VMEM((ITERS, 2 * SITES, ROWS, M), F32),
            pltpu.VMEM((BDEV, ROWS, M), F32),
            pltpu.VMEM((POOL, ROWS, M), F32),
            pltpu.VMEM((POOL, ROWS, M), F32),
            pltpu.VMEM((POOL, ROWS, M), F32),
            pltpu.VMEM((BDEV, ROWS, M), F32),
            pltpu.VMEM((SITES, ROWS, M), F32),
            pltpu.VMEM((SITES, ROWS, M), F32),
            pltpu.SemaphoreType.DMA((2,)),
            pltpu.SemaphoreType.DMA((ITERS,)),
            pltpu.SemaphoreType.DMA((ITERS,)),
            pltpu.SemaphoreType.DMA((2,)),
            pltpu.SemaphoreType.DMA((2,)),
        ],
        compiler_params=pltpu.CompilerParams(
            collective_id=0, has_side_effects=True, vmem_limit_bytes=48 * 1024 * 1024
        ),
        cost_estimate=pl.CostEstimate(
            flops=3_000_000_000, bytes_accessed=6_000_000, transcendentals=0
        ),
    )(
        incident.reshape(BDEV, ROWS, M),
        diffraction,
        mixing,
        coupling.reshape(BDEV, 2 * K, M),
        lists.reshape(1, 1, BDEV * K),
        groups.reshape(1, BDEV),
        jacket.reshape(2, M, NF),
    )
    return coef.reshape(BDEV, 4, 2, M), resp.reshape(1, 4, 2, NF)


def solution(mesh):
    placed = (
        P("site", "freq", None, None),
        P("freq", None, None),
        P("freq", None, None),
        P("site", "freq", None, None),
        P("site", None),
        P("site", None),
        P("site", "freq", None, None),
    )
    return jax.shard_map(
        per_device,
        mesh=mesh,
        in_specs=placed,
        out_specs=(P("site", "freq", None, None), P("site", "freq", None, None)),
        check_vma=False,
    )
```

```python
import jax
import jax.numpy as jnp
from jax import lax
from jax.experimental import pallas as pl
from jax.experimental.pallas import tpu as pltpu
from jax.sharding import PartitionSpec as P

ITERS = 3
NZ = 8
NX = 4
SITES = NZ * NX
BDEV = 16
K = 8
M = 512
HALF = M // 2
NF = 128
ROWS = 8
TEAMS = 2
POOL = 2 * SITES + BDEV
LOCAL = 6
MESH = pl.DeviceIdType.MESH
F32 = jnp.float32
BF16 = jnp.bfloat16


def split(x):
    hi = x.astype(BF16)
    lo = (x - hi.astype(F32)).astype(BF16)
    return hi, lo


def turn(x):
    n = x.shape[0]
    even = lax.broadcasted_iota(jnp.int32, x.shape, 0) % 2 == 0
    return jnp.where(even, -pltpu.roll(x, n - 1, 0), pltpu.roll(x, 1, 0))


def product(x, w_hi, w_lo):
    rows, width = x.shape[0], w_hi.shape[1] // 2
    x_hi, x_lo = split(x)
    y = jnp.dot(jnp.concatenate([x_hi, x_lo], axis=0), w_hi[...], preferred_element_type=F32)
    y = y[:rows] + y[rows:] + jnp.dot(x_hi, w_lo[...], preferred_element_type=F32)
    return y[:, :width] + turn(y[:, width:])


def load_matrix(src, w_hi, w_lo):
    width = src.shape[2]
    for part in range(2):
        hi, lo = split(src[part])
        w_hi[:, part * width : (part + 1) * width] = hi
        w_lo[:, part * width : (part + 1) * width] = lo


def swap_halves(a, b):
    upper = lax.broadcasted_iota(jnp.int32, a.shape, 1) < ROWS // 2
    first = jnp.where(upper, a, pltpu.roll(b, ROWS // 2, 1))
    second = jnp.where(upper, pltpu.roll(a, ROWS // 2, 1), b)
    return first, second


def to_rows(tiles):
    pairs = tiles.reshape(BDEV // 2, 2, ROWS, HALF)
    low, high = swap_halves(pairs[:, 0], pairs[:, 1])
    return jnp.concatenate([low, high], axis=-1).reshape(BDEV * ROWS // 2, M)


def store_tiles(out, rows):
    rows = rows.reshape(BDEV // 2, ROWS, M)
    even, odd = swap_halves(rows[:, :, :HALF], rows[:, :, HALF:])
    for pair in range(BDEV // 2):
        out[2 * pair] = even[pair]
        out[2 * pair + 1] = odd[pair]


def kernel(*refs):
    refs = list(refs)

    def take(count):
        taken = refs[:count]
        del refs[:count]
        return taken

    incident_h, diffraction_h, mixing_h, coupling_h, lists, groups, jacket_h = take(7)
    coef_out, resp_out = take(2)
    incident_v, diffraction_v, mixing_v, coupling_v, jacket_v = take(5)
    d_hi, d_lo, m_hi, m_lo, j_hi, j_lo = take(6)
    incident, factor, incoming, result, own = take(5)
    lists_all, picks, places, picks_s, places_s = take(5)
    sending, shares, totals = take(3)
    pools = [take(TEAMS) for _ in range(ITERS)]
    relays = [[take(2) for _ in range(TEAMS)] for _ in range(ITERS)]
    in_sems, list_sems, dense_send, dense_recv, row_send, row_recv, share_send, share_recv, table_sem = take(9)

    me = lax.axis_index("site")
    z, x = me // NX, me % NX

    def at(dz, dx):
        return ((z + dz + NZ) % NZ) * NX + (x + dx) % NX

    def send(src, dst, send_sem, recv_sem, site):
        pltpu.make_async_remote_copy(
            src_ref=src,
            dst_ref=dst,
            send_sem=send_sem,
            recv_sem=recv_sem,
            device_id={"site": site},
            device_id_type=MESH,
        ).start()

    def done(ref, sem):
        pltpu.make_async_copy(ref, ref, sem).wait()

    def place_of(behind, aside):
        return aside * NZ + (behind + 1) % NZ

    loads = [
        pltpu.make_async_copy(src, dst, in_sems.at[i])
        for i, (src, dst) in enumerate(
            (
                (incident_h, incident_v),
                (diffraction_h, diffraction_v),
                (mixing_h, mixing_v),
                (coupling_h, coupling_v),
                (jacket_h, jacket_v),
            )
        )
    ]
    for load in loads:
        load.start()

    barrier = pltpu.get_barrier_semaphore()

    @pl.loop(1, SITES)
    def _(step):
        site = at(step // NX, step % NX)
        pl.semaphore_signal(barrier, inc=1, device_id={"site": site}, device_id_type=MESH)

    loads[0].wait()
    heads = incident_v[...]
    first, second = swap_halves(heads[:, :, :HALF], heads[:, :, HALF:])
    incident[0] = first
    incident[1] = second
    loads[1].wait()
    load_matrix(diffraction_v, d_hi, d_lo)
    loads[2].wait()
    load_matrix(mixing_v, m_hi, m_lo)

    def outgoing_of(sweep, team, tiles):
        coef = product(to_rows(tiles), d_hi, d_lo)
        store_tiles(own.at[sweep, team], product(coef, m_hi, m_lo))

    for team in range(TEAMS):
        outgoing_of(0, team, incident[team])

    own_list = lists[0]
    owner = own_list // BDEV
    local = own_list % BDEV
    sites = lax.broadcasted_iota(jnp.int32, (SITES, BDEV * K), 0)
    named = owner == sites
    last = jnp.max(jnp.where(named, local, -1), axis=1, keepdims=True)
    later = jnp.max(jnp.where(named & (local == last), 1, 0), axis=0, keepdims=True)
    behind = (z - owner // NX + NZ) % NZ
    aside = (x - owner % NX + NX) % NX
    places[...] = jnp.where(owner == me, 2 * SITES + local, 2 * place_of(behind, aside) + later)
    move_places = pltpu.make_async_copy(places, places_s, table_sem.at[0])
    move_places.start()
    lists_all[0] = lists[0]

    loads[3].wait()
    tile_upper = lax.broadcasted_iota(jnp.int32, (ROWS, HALF), 0) < ROWS // 2

    @pl.loop(0, BDEV)
    def _(body):
        for k in range(2 * K):
            factor[body, k] = jnp.where(
                tile_upper,
                coupling_v[body, k : k + 1, :HALF],
                coupling_v[body, k : k + 1, HALF:],
            )

    loads[4].wait()
    load_matrix(jacket_v, j_hi, j_lo)

    pl.semaphore_wait(barrier, SITES - 1)

    def send_dense(sweep, team):
        for way, step in enumerate((1, -1)):
            send(
                own.at[sweep, team],
                relays[sweep][team][way],
                dense_send.at[sweep, team],
                dense_recv.at[sweep, team, way],
                at(step, 0),
            )

    def send_aside(sweep, team):
        for dx in range(1, NX):
            row = 2 * place_of(0, dx)
            for i in range(2):
                sending[sweep, team, row + i] = own[sweep, team, picks_s[dx, i]]
            send(
                sending.at[sweep, team, pl.ds(row, 2)],
                pools[sweep][team].at[pl.ds(row, 2)],
                row_send.at[sweep, team],
                row_recv.at[sweep, team],
                at(0, dx),
            )

    def pass_on(sweep, team):
        pool = pools[sweep][team]
        for way in range(2):
            done(relays[sweep][team][way], dense_recv.at[sweep, team, way])

        def forward(way, hop, dx, number, skip):
            step = (1, -1)[way]
            block = relays[sweep][team][way]
            row = 2 * place_of((step * (hop + 1) + NZ) % NZ, dx) + skip
            entry = ((step * hop + NZ) % NZ) * NX + dx
            for i in range(number):
                sending[sweep, team, row + i] = block[picks_s[entry, 2 + 2 * way + skip + i]]
            send(
                sending.at[sweep, team, pl.ds(row, number)],
                pool.at[pl.ds(row, number)],
                row_send.at[sweep, team],
                row_recv.at[sweep, team],
                at(step * hop, dx),
            )

        @pl.loop(0, NX)
        def _(dx):
            for way in range(2):
                forward(way, NZ // 2 - 1, dx, 1, way)

        @pl.loop(0, 3 * NX - 1)
        def _(i):
            item = 3 * NX - 1 - i
            for way in range(2):
                forward(way, item // NX, item % NX, 2, 0)

        pool[2 * SITES :] = own[sweep, team]
        for way in range(2):
            row = 2 * place_of((1, NZ - 1)[way], 0)
            for i in range(2):
                pool[row + i] = relays[sweep][team][way][picks_s[0, 2 + 2 * way + i]]

    def gather(sweep, team):
        pool = pools[sweep][team]
        done(pool.at[pl.ds(LOCAL, 2 * SITES - LOCAL)], row_recv.at[sweep, team])

        @pl.loop(0, BDEV)
        def _(body):
            straight = incident[team, body]
            turned = jnp.zeros((ROWS, HALF), F32)
            for k in range(K):
                value = pool[places_s[0, body * K + k]]
                straight = straight + factor[body, 2 * k] * value
                turned = turned + factor[body, 2 * k + 1] * value
            incoming[team, body] = straight + turn(turned)

    def share_of(team, site):
        share = jnp.zeros((ROWS, HALF), F32)
        for body in range(BDEV):
            share = share + jnp.where(groups[0, body] == site, 1.0, 0.0) * incoming[team, body]
        return share

    def send_shares(team):
        @pl.loop(1, SITES)
        def _(step):
            site = at(step // NX, step % NX)
            shares[team, step] = share_of(team, site)
            send(
                shares.at[team, step],
                totals.at[team, step],
                share_send.at[team],
                share_recv.at[team],
                site,
            )

    @pl.loop(1, SITES)
    def _(step):
        dz, dx = step // NX, step % NX
        send(
            lists.at[0],
            lists_all.at[((NZ - dz) % NZ) * NX + (NX - dx) % NX],
            list_sems.at[0],
            list_sems.at[1],
            at(dz, dx),
        )

    for team in range(TEAMS):
        send_dense(0, team)

    done(lists_all.at[1:], list_sems.at[1])
    everyone = lists_all[:, 0, :]
    lane = lax.broadcasted_iota(jnp.int32, (SITES, 128), 1)
    table = jnp.zeros((SITES, 128), jnp.int32)
    for i, source in enumerate((me, at(-1, 0), at(1, 0))):
        theirs = everyone // BDEV == source
        wanted = everyone % BDEV
        smallest = jnp.min(jnp.where(theirs, wanted, BDEV - 1), axis=1, keepdims=True)
        largest = jnp.max(jnp.where(theirs, wanted, 0), axis=1, keepdims=True)
        table = jnp.where(lane == 2 * i, smallest, table)
        table = jnp.where(lane == 2 * i + 1, largest, table)
    picks[...] = table
    move_picks = pltpu.make_async_copy(picks, picks_s, table_sem.at[1])
    move_picks.start()
    move_places.wait()
    move_picks.wait()

    for sweep in range(ITERS):
        if sweep == 0:
            for team in range(TEAMS):
                send_aside(sweep, team)
        for team in range(TEAMS):
            pass_on(sweep, team)
        if sweep < ITERS - 1:
            for team in range(TEAMS):
                gather(sweep, team)
                outgoing_of(sweep + 1, team, incoming[team])
                send_dense(sweep + 1, team)
                send_aside(sweep + 1, team)

    for team in range(TEAMS):
        gather(ITERS - 1, team)
        send_shares(team)
        store_tiles(result.at[team], product(to_rows(incoming[team]), d_hi, d_lo))
    low, high = swap_halves(result[0], result[1])
    coef_out[:, :, :HALF] = low
    coef_out[:, :, HALF:] = high

    sums = []
    for team in range(TEAMS):
        total = share_of(team, me)
        done(totals.at[team, pl.ds(1, SITES - 1)], share_recv.at[team])
        for step in range(1, SITES):
            total = total + totals[team, step]
        sums.append(total[None])
    low, high = swap_halves(sums[0], sums[1])
    total = jnp.concatenate([low[0], high[0]], axis=-1)
    resp_out[...] = product(product(total, d_hi, d_lo), j_hi, j_lo)

    done(lists_all.at[1:], list_sems.at[0])
    for team in range(TEAMS):
        for sweep in range(ITERS):
            for _ in range(2):
                done(own.at[sweep, team], dense_send.at[sweep, team])
            done(sending.at[sweep, team, pl.ds(LOCAL, 2 * SITES - LOCAL)], row_send.at[sweep, team])
        done(shares.at[team, pl.ds(1, SITES - 1)], share_send.at[team])


def per_device(incident, diffraction, mixing, coupling, lists, groups, jacket):
    vmem = pl.BlockSpec(memory_space=pltpu.VMEM)
    smem = pl.BlockSpec(memory_space=pltpu.SMEM)
    anywhere = pl.BlockSpec(memory_space=pl.ANY)

    def f32(*shape):
        return pltpu.VMEM(shape, F32)

    def dma(*shape):
        return pltpu.SemaphoreType.DMA(shape)

    coef, resp = pl.pallas_call(
        kernel,
        out_shape=(
            jax.ShapeDtypeStruct((BDEV, ROWS, M), F32),
            jax.ShapeDtypeStruct((ROWS, NF), F32),
        ),
        in_specs=[anywhere] * 4 + [vmem, smem, anywhere],
        out_specs=(vmem, vmem),
        scratch_shapes=[
            f32(BDEV, ROWS, M),
            f32(2, M, M),
            f32(2, M, M),
            f32(BDEV, 2 * K, M),
            f32(2, M, NF),
            *[pltpu.VMEM((M, 2 * M), BF16)] * 4,
            *[pltpu.VMEM((M, 2 * NF), BF16)] * 2,
            f32(TEAMS, BDEV, ROWS, HALF),
            f32(BDEV, 2 * K, ROWS, HALF),
            f32(TEAMS, BDEV, ROWS, HALF),
            f32(TEAMS, BDEV, ROWS, HALF),
            f32(ITERS, TEAMS, BDEV, ROWS, HALF),
            pltpu.VMEM((SITES, 1, BDEV * K), jnp.int32),
            pltpu.VMEM((SITES, 128), jnp.int32),
            pltpu.VMEM((1, 128), jnp.int32),
            pltpu.SMEM((SITES, 128), jnp.int32),
            pltpu.SMEM((1, 128), jnp.int32),
            f32(ITERS, TEAMS, 2 * SITES, ROWS, HALF),
            f32(TEAMS, SITES, ROWS, HALF),
            f32(TEAMS, SITES, ROWS, HALF),
            *[f32(POOL, ROWS, HALF)] * (ITERS * TEAMS),
            *[f32(BDEV, ROWS, HALF)] * (ITERS * TEAMS * 2),
            dma(5),
            dma(2),
            dma(ITERS, TEAMS),
            dma(ITERS, TEAMS, 2),
            dma(ITERS, TEAMS),
            dma(ITERS, TEAMS),
            dma(TEAMS),
            dma(TEAMS),
            dma(2),
        ],
        compiler_params=pltpu.CompilerParams(
            collective_id=0, has_side_effects=True, vmem_limit_bytes=52 * 1024 * 1024
        ),
        cost_estimate=pl.CostEstimate(
            flops=3_000_000_000, bytes_accessed=6_000_000, transcendentals=0
        ),
    )(
        incident.reshape(BDEV, ROWS, M),
        diffraction,
        mixing,
        coupling.reshape(BDEV, 2 * K, M),
        lists.reshape(1, 1, BDEV * K),
        groups.reshape(1, BDEV),
        jacket.reshape(2, M, NF),
    )
    return coef.reshape(BDEV, 4, 2, M), resp.reshape(1, 4, 2, NF)


def solution(mesh):
    placed = (
        P("site", "freq", None, None),
        P("freq", None, None),
        P("freq", None, None),
        P("site", "freq", None, None),
        P("site", None),
        P("site", None),
        P("site", "freq", None, None),
    )
    return jax.shard_map(
        per_device,
        mesh=mesh,
        in_specs=placed,
        out_specs=(P("site", "freq", None, None), P("site", "freq", None, None)),
        check_vma=False,
    )
```

```python
import jax
import jax.numpy as jnp
from jax import lax
from jax.experimental import pallas as pl
from jax.experimental.pallas import tpu as pltpu
from jax.sharding import PartitionSpec as P

ITERS = 3
NZ = 8
NX = 4
SITES = NZ * NX
BDEV = 16
K = 8
M = 512
LANES = 128
QUADS = M // LANES
NF = 128
ROWS = 8
TEAMS = 4
POOL = 2 * SITES + BDEV
LOCAL = 10
WAYS = (1, -1)
MESH = pl.DeviceIdType.MESH
F32 = jnp.float32
BF16 = jnp.bfloat16


def split(x):
    hi = x.astype(BF16)
    lo = (x - hi.astype(F32)).astype(BF16)
    return hi, lo


def is_real(shape):
    return lax.broadcasted_iota(jnp.int32, shape, 0) % 2 == 0


def turn(x):
    n = x.shape[0]
    return jnp.where(is_real(x.shape), -pltpu.roll(x, n - 1, 0), pltpu.roll(x, 1, 0))


def product(x, w_hi, w_lo):
    rows, width = x.shape[0], w_hi.shape[1] // 2
    x_hi, x_lo = split(x)
    y = jnp.dot(jnp.concatenate([x_hi, x_lo], axis=0), w_hi[...], preferred_element_type=F32)
    y = y[:rows] + y[rows:] + jnp.dot(x_hi, w_lo[...], preferred_element_type=F32)
    return y[:, :width] + turn(y[:, width:])


def load_matrix(src, w_hi, w_lo):
    width = src.shape[2]
    for part in range(2):
        hi, lo = split(src[part])
        w_hi[:, part * width : (part + 1) * width] = hi
        w_lo[:, part * width : (part + 1) * width] = lo


def exchange(a, b, span):
    even = lax.broadcasted_iota(jnp.int32, a.shape, 1) // span % 2 == 0
    first = jnp.where(even, a, pltpu.roll(b, span, 1))
    second = jnp.where(even, pltpu.roll(a, ROWS - span, 1), b)
    return first, second


def transpose_quads(tiles):
    t0, t2 = exchange(tiles[0], tiles[2], 4)
    t1, t3 = exchange(tiles[1], tiles[3], 4)
    return (*exchange(t0, t1, 2), *exchange(t2, t3, 2))


def to_rows(tiles):
    count = tiles.shape[0]
    fours = tiles.reshape(count // 4, 4, ROWS, LANES)
    blocks = transpose_quads([fours[:, i] for i in range(4)])
    return jnp.concatenate(blocks, axis=-1).reshape(count * 2, M)


def to_tiles(rows):
    stacked = rows.reshape(rows.shape[0] // ROWS, ROWS, M)
    blocks = [stacked[:, :, q * LANES : (q + 1) * LANES] for q in range(QUADS)]
    fours = transpose_quads(blocks)
    return [fours[body % 4][body // 4] for body in range(rows.shape[0] // 2)]


def kernel(*refs):
    refs = list(refs)

    def take(count):
        taken = refs[:count]
        del refs[:count]
        return taken

    incident_h, diffraction_h, mixing_h, coupling_h, lists_h, groups_h, jacket_h = take(7)
    coef_out, resp_out = take(2)
    incident, diffraction_v, mixing_v, coupling_v, jacket_v, lists, groups = take(7)
    d_hi, d_lo, m_hi, m_lo, j_hi, j_lo = take(6)
    factor, incoming, own = take(3)
    lists_all, picks, places, named_by, member, picks_s, places_s = take(7)
    sending, shares, aside_parts, totals = take(4)
    pools = [take(TEAMS) for _ in range(ITERS)]
    near = [[take(2) for _ in range(TEAMS)] for _ in range(ITERS)]
    far = [[take(2) for _ in range(TEAMS)] for _ in range(ITERS)]
    in_sems, list_sems, dense_send, near_recv, far_recv, row_send, row_recv, part_sems, share_sems, table_sem = take(10)

    me = lax.axis_index("site")
    z, x = me // NX, me % NX

    z_parts = [(z + dz) % NZ * NX for dz in range(NZ)]
    x_parts = [(x + dx) % NX for dx in range(NX)]

    def at(dz, dx):
        return z_parts[dz % NZ] + x_parts[dx % NX]

    def send(src, dst, send_sem, recv_sem, site):
        pltpu.make_async_remote_copy(
            src_ref=src,
            dst_ref=dst,
            send_sem=send_sem,
            recv_sem=recv_sem,
            device_id={"site": site},
            device_id_type=MESH,
        ).start()

    def done(ref, sem):
        pltpu.make_async_copy(ref, ref, sem).wait()

    def place_of(behind, aside):
        return aside * NZ + (behind + 2) % NZ

    def outgoing_of(sweep, team, tiles):
        coef = product(to_rows(tiles), d_hi, d_lo)
        for body, tile in enumerate(to_tiles(product(coef, m_hi, m_lo))):
            own[sweep, team, body] = tile

    def send_dense(sweep, team):
        for way, step in enumerate(WAYS):
            send(
                own.at[sweep, team],
                near[sweep][team][way],
                dense_send.at[sweep, team],
                near_recv.at[sweep, team, way],
                at(step, 0),
            )

    def send_picked(sweep, team, block, dz, dx, behind, lane, number, skip):
        row = 2 * place_of((behind + NZ) % NZ, dx) + skip
        entry = ((dz + NZ) % NZ) * NX + dx
        for i in range(number):
            sending[sweep, team, row + i] = block[picks_s[entry, lane + skip + i]]
        send(
            sending.at[sweep, team, pl.ds(row, number)],
            pools[sweep][team].at[pl.ds(row, number)],
            row_send.at[sweep, team],
            row_recv.at[sweep, team],
            at(dz, dx),
        )

    def send_aside(sweep, team):
        for dx in range(1, NX):
            send_picked(sweep, team, own.at[sweep, team], 0, dx, 0, 0, 2, 0)

    def pass_near(sweep, team):
        for way, step in enumerate(WAYS):
            done(near[sweep][team][way], near_recv.at[sweep, team, way])
            send(
                near[sweep][team][way],
                far[sweep][team][way],
                dense_send.at[sweep, team],
                far_recv.at[sweep, team, way],
                at(step, 0),
            )

        for dx in range(1, NX):
            for way, step in enumerate(WAYS):
                send_picked(sweep, team, near[sweep][team][way], 0, dx, step, 2 + 2 * way, 2, 0)

    def pass_far(sweep, team):
        for way in range(2):
            done(far[sweep][team][way], far_recv.at[sweep, team, way])

        for dx in range(NX):
            for way, step in enumerate(WAYS):
                send_picked(sweep, team, far[sweep][team][way], 2 * step, dx, 4 * step, 6 + 2 * way, 1, way)

        for item in range(2 * NX - 1, 0, -1):
            hop, dx = item // NX, item % NX
            for way, step in enumerate(WAYS):
                send_picked(
                    sweep, team, far[sweep][team][way], step * hop, dx, step * (hop + 2), 6 + 2 * way, 2, 0
                )

        pool = pools[sweep][team]
        pool[2 * SITES :] = own[sweep, team]
        for way, step in enumerate(WAYS):
            for distance, blocks in ((1, near), (2, far)):
                row = 2 * place_of((step * distance + NZ) % NZ, 0)
                for i in range(2):
                    pool[row + i] = blocks[sweep][team][way][picks_s[0, 4 * distance - 2 + 2 * way + i]]

    def gather(sweep, team):
        pool = pools[sweep][team]
        done(pool.at[pl.ds(LOCAL, 2 * SITES - LOCAL)], row_recv.at[sweep, team])

        @pl.loop(0, BDEV // 4)
        def _(four):
            for i in range(4):
                body = 4 * four + i
                straight = incident[body, team]
                turned = jnp.zeros((ROWS, LANES), F32)
                for k in range(K):
                    value = pool[places_s[k, body]]
                    straight = straight + factor[body, 2 * k] * value
                    turned = turned + factor[body, 2 * k + 1] * value
                incoming[team, body] = straight + turn(turned)

    def share_parts(team):
        bodies = [incoming[team, body] for body in range(BDEV)]

        @pl.loop(0, SITES // 8)
        def _(eight):
            for i in range(8):
                item = eight * 8 + i
                share = member[item, 0:1, :] * bodies[0]
                for body in range(1, BDEV):
                    share = share + member[item, body : body + 1, :] * bodies[body]
                shares[team, item] = share

        for dx in range(1, NX):
            send(
                shares.at[team, pl.ds(dx * NZ, NZ)],
                aside_parts.at[team, pl.ds(dx * NZ, NZ)],
                part_sems.at[0, team],
                part_sems.at[1, team],
                at(0, dx),
            )

    def share_totals(team):
        done(aside_parts.at[team, pl.ds(NZ, SITES - NZ)], part_sems.at[1, team])
        total = shares[team, pl.ds(0, NZ)]
        for dx in range(1, NX):
            total = total + aside_parts[team, pl.ds(dx * NZ, NZ)]
        totals[team, 0] = total
        for dz in range(1, NZ):
            send(
                totals.at[team, 0, dz],
                totals.at[team, 1, dz],
                share_sems.at[0, team],
                share_sems.at[1, team],
                at(dz, 0),
            )

    def store_coefficients(team):
        rows = product(to_rows(incoming[team]), d_hi, d_lo)
        for body, tile in enumerate(to_tiles(rows)):
            coef_out[body, team] = tile

    barrier = pltpu.get_barrier_semaphore()

    for step in range(1, SITES):
        site = at(step // NX, step % NX)
        pl.semaphore_signal(barrier, inc=1, device_id={"site": site}, device_id_type=MESH)

    loads = [
        pltpu.make_async_copy(src, dst, in_sems.at[i])
        for i, (src, dst) in enumerate(
            (
                (incident_h, incident),
                (diffraction_h, diffraction_v),
                (mixing_h, mixing_v),
                (coupling_h, coupling_v),
                (jacket_h, jacket_v),
                (lists_h, lists),
                (groups_h, groups),
            )
        )
    ]
    for load in loads:
        load.start()

    loads[1].wait()
    load_matrix(diffraction_v, d_hi, d_lo)
    loads[2].wait()
    load_matrix(mixing_v, m_hi, m_lo)
    loads[0].wait()
    for team in range(TEAMS):
        outgoing_of(0, team, incident[:, team])

    loads[5].wait()
    own_list = lists[...]
    owner = own_list // BDEV
    local = own_list % BDEV
    sites = lax.broadcasted_iota(jnp.int32, (SITES, K, BDEV), 0)
    named = owner[None] == sites
    last = jnp.where(named, local[None], -1)
    last = jnp.max(jnp.max(last, axis=1, keepdims=True), axis=2, keepdims=True)
    later = jnp.max(jnp.where(named & (local[None] == last), 1, 0), axis=0)
    behind = (z - owner // NX + NZ) % NZ
    aside = (x - owner % NX + NX) % NX
    places[...] = jnp.zeros((K, 128), jnp.int32)
    places[:, :BDEV] = jnp.where(owner == me, 2 * SITES + local, 2 * place_of(behind, aside) + later)
    move_places = pltpu.make_async_copy(places, places_s, table_sem.at[0])
    move_places.start()
    lists_all[0] = own_list

    loads[3].wait()
    real = is_real((ROWS, LANES))

    @pl.loop(0, BDEV)
    def _(body):
        for k in range(K):
            both = coupling_v[body, k]
            factor[body, 2 * k] = jnp.where(real, both, pltpu.roll(both, 1, 0))
            factor[body, 2 * k + 1] = jnp.where(real, pltpu.roll(both, ROWS - 1, 0), both)

    loads[4].wait()
    load_matrix(jacket_v, j_hi, j_lo)
    halves = []
    for part in range(2):
        columns = pl.ds(part * M, M)
        both = jnp.dot(d_hi[:, columns], j_hi[...], preferred_element_type=F32)
        both = both + jnp.dot(d_lo[:, columns], j_hi[...], preferred_element_type=F32)
        halves.append(both + jnp.dot(d_hi[:, columns], j_lo[...], preferred_element_type=F32))
    joint_real = halves[0][:, :NF] - halves[1][:, NF:]
    joint_imag = halves[0][:, NF:] + halves[1][:, :NF]
    j_hi[:, :NF], j_lo[:, :NF] = split(joint_real)
    j_hi[:, NF:], j_lo[:, NF:] = split(joint_imag)

    loads[6].wait()
    for body in range(BDEV):
        named_by[body : body + 1, :] = jnp.full((1, LANES), groups[0, body], jnp.int32)

    for item in range(SITES):
        member[item] = jnp.where(named_by[...] == at(item % NZ, item // NZ), 1.0, 0.0)

    pl.semaphore_wait(barrier, SITES - 1)

    send_dense(0, 0)
    for step in range(1, SITES):
        dz, dx = step // NX, step % NX
        send(
            lists,
            lists_all.at[((NZ - dz) % NZ) * NX + (NX - dx) % NX],
            list_sems.at[0],
            list_sems.at[1],
            at(dz, dx),
        )

    for team in range(1, TEAMS):
        send_dense(0, team)

    done(lists_all.at[1:], list_sems.at[1])
    everyone = lists_all[...]
    lane = lax.broadcasted_iota(jnp.int32, (SITES, 128), 1)
    table = jnp.zeros((SITES, 128), jnp.int32)
    for i, dz in enumerate((0, -1, 1, -2, 2)):
        theirs = everyone // BDEV == at(dz, 0)
        wanted = everyone % BDEV
        smallest = jnp.min(jnp.where(theirs, wanted, BDEV - 1), axis=1)
        largest = jnp.max(jnp.where(theirs, wanted, 0), axis=1)
        table = jnp.where(lane == 2 * i, jnp.min(smallest, axis=1, keepdims=True), table)
        table = jnp.where(lane == 2 * i + 1, jnp.max(largest, axis=1, keepdims=True), table)
    picks[...] = table
    move_picks = pltpu.make_async_copy(picks, picks_s, table_sem.at[1])
    move_picks.start()
    move_places.wait()
    move_picks.wait()

    for sweep in range(ITERS):
        if sweep == 0:
            for team in range(TEAMS):
                send_aside(sweep, team)
        for team in range(TEAMS):
            pass_near(sweep, team)
        for team in range(TEAMS):
            pass_far(sweep, team)
        if sweep < ITERS - 1:
            for team in range(TEAMS):
                gather(sweep, team)
                outgoing_of(sweep + 1, team, incoming[team])
                send_dense(sweep + 1, team)
                send_aside(sweep + 1, team)

    for team in range(TEAMS):
        gather(ITERS - 1, team)
        share_parts(team)
        if team > 0:
            share_totals(team - 1)
        store_coefficients(team)
    share_totals(TEAMS - 1)

    sums = []
    for team in range(TEAMS):
        done(totals.at[team, 1, pl.ds(1, NZ - 1)], share_sems.at[1, team])
        total = totals[team, 0, 0]
        for dz in range(1, NZ):
            total = total + totals[team, 1, dz]
        sums.append(total[None])
    total = jnp.concatenate(transpose_quads(sums), axis=-1)[0]
    resp_out[...] = product(total, j_hi, j_lo)

    done(lists_all.at[1:], list_sems.at[0])
    for team in range(TEAMS):
        for sweep in range(ITERS):
            for way in range(2):
                done(own.at[sweep, team], dense_send.at[sweep, team])
                done(near[sweep][team][way], dense_send.at[sweep, team])
            done(sending.at[sweep, team, pl.ds(LOCAL, 2 * SITES - LOCAL)], row_send.at[sweep, team])
        done(shares.at[team, pl.ds(NZ, SITES - NZ)], part_sems.at[0, team])
        done(totals.at[team, 0, pl.ds(1, NZ - 1)], share_sems.at[0, team])


def to_native(values):
    lead = values.shape[:-2]
    return jnp.swapaxes(values.reshape(*lead, 2, QUADS, LANES), -3, -2).reshape(*lead, ROWS, LANES)


def from_native(tiles):
    lead = tiles.shape[:-2]
    return jnp.swapaxes(tiles.reshape(*lead, QUADS, 2, LANES), -3, -2).reshape(*lead, 2, M)


def per_device(incident, diffraction, mixing, coupling, lists, groups, jacket):
    vmem = pl.BlockSpec(memory_space=pltpu.VMEM)
    anywhere = pl.BlockSpec(memory_space=pl.ANY)

    def f32(*shape):
        return pltpu.VMEM(shape, F32)

    def i32(*shape):
        return pltpu.VMEM(shape, jnp.int32)

    def dma(*shape):
        return pltpu.SemaphoreType.DMA(shape)

    coef, resp = pl.pallas_call(
        kernel,
        out_shape=(
            jax.ShapeDtypeStruct((BDEV, TEAMS, ROWS, LANES), F32),
            jax.ShapeDtypeStruct((ROWS, NF), F32),
        ),
        in_specs=[anywhere] * 7,
        out_specs=(vmem, vmem),
        scratch_shapes=[
            f32(BDEV, TEAMS, ROWS, LANES),
            f32(2, M, M),
            f32(2, M, M),
            f32(BDEV, K, ROWS, LANES),
            f32(2, M, NF),
            i32(K, BDEV),
            pltpu.SMEM((1, BDEV), jnp.int32),
            *[pltpu.VMEM((M, 2 * M), BF16)] * 4,
            *[pltpu.VMEM((M, 2 * NF), BF16)] * 2,
            f32(BDEV, 2 * K, ROWS, LANES),
            f32(TEAMS, BDEV, ROWS, LANES),
            f32(ITERS, TEAMS, BDEV, ROWS, LANES),
            i32(SITES, K, BDEV),
            i32(SITES, 128),
            i32(K, 128),
            i32(BDEV, LANES),
            f32(SITES, BDEV, LANES),
            pltpu.SMEM((SITES, 128), jnp.int32),
            pltpu.SMEM((K, 128), jnp.int32),
            f32(ITERS, TEAMS, 2 * SITES, ROWS, LANES),
            f32(TEAMS, SITES, ROWS, LANES),
            f32(TEAMS, SITES, ROWS, LANES),
            f32(TEAMS, 2, NZ, ROWS, LANES),
            *[f32(POOL, ROWS, LANES)] * (ITERS * TEAMS),
            *[f32(BDEV, ROWS, LANES)] * (ITERS * TEAMS * 4),
            dma(7),
            dma(2),
            dma(ITERS, TEAMS),
            dma(ITERS, TEAMS, 2),
            dma(ITERS, TEAMS, 2),
            dma(ITERS, TEAMS),
            dma(ITERS, TEAMS),
            dma(2, TEAMS),
            dma(2, TEAMS),
            dma(2),
        ],
        compiler_params=pltpu.CompilerParams(
            collective_id=0, has_side_effects=True, vmem_limit_bytes=44 * 1024 * 1024
        ),
        cost_estimate=pl.CostEstimate(
            flops=3_000_000_000, bytes_accessed=6_000_000, transcendentals=0
        ),
    )(
        *[
            pltpu.with_memory_space_constraint(operand, pltpu.HBM)
            for operand in (
                to_native(incident),
                diffraction,
                mixing,
                to_native(coupling),
                lists.T,
                groups.reshape(1, BDEV),
                jacket.reshape(2, M, NF),
            )
        ]
    )
    return from_native(coef), resp.reshape(1, 4, 2, NF)


def solution(mesh):
    placed = (
        P("site", "freq", None, None),
        P("freq", None, None),
        P("freq", None, None),
        P("site", "freq", None, None),
        P("site", None),
        P("site", None),
        P("site", "freq", None, None),
    )
    return jax.shard_map(
        per_device,
        mesh=mesh,
        in_specs=placed,
        out_specs=(P("site", "freq", None, None), P("site", "freq", None, None)),
        check_vma=False,
    )
```

```python
import jax
import jax.numpy as jnp
from jax import lax
from jax.experimental import pallas as pl
from jax.experimental.pallas import tpu as pltpu
from jax.sharding import PartitionSpec as P

ITERS = 3
NZ = 8
NX = 4
SITES = NZ * NX
BDEV = 16
K = 8
M = 512
LANES = 128
QUADS = M // LANES
NF = 128
ROWS = 8
TEAMS = 4
POOL = 2 * SITES + BDEV
LOCAL = 10
WAYS = (1, -1)
MESH = pl.DeviceIdType.MESH
F32 = jnp.float32
BF16 = jnp.bfloat16


def split(x):
    hi = x.astype(BF16)
    lo = (x - hi.astype(F32)).astype(BF16)
    return hi, lo


def is_real(shape):
    return lax.broadcasted_iota(jnp.int32, shape, 0) % 2 == 0


def turn(x):
    n = x.shape[0]
    return jnp.where(is_real(x.shape), -pltpu.roll(x, n - 1, 0), pltpu.roll(x, 1, 0))


def product(x, w_hi, w_lo):
    rows, width = x.shape[0], w_hi.shape[1] // 2
    x_hi, x_lo = split(x)
    y = jnp.dot(jnp.concatenate([x_hi, x_lo], axis=0), w_hi[...], preferred_element_type=F32)
    y = y[:rows] + y[rows:] + jnp.dot(x_hi, w_lo[...], preferred_element_type=F32)
    return y[:, :width] + turn(y[:, width:])


def load_matrix(src, w_hi, w_lo):
    width = src.shape[2]
    for part in range(2):
        hi, lo = split(src[part])
        w_hi[:, part * width : (part + 1) * width] = hi
        w_lo[:, part * width : (part + 1) * width] = lo


def exchange(a, b, span):
    even = lax.broadcasted_iota(jnp.int32, a.shape, 1) // span % 2 == 0
    first = jnp.where(even, a, pltpu.roll(b, span, 1))
    second = jnp.where(even, pltpu.roll(a, ROWS - span, 1), b)
    return first, second


def transpose_quads(tiles):
    t0, t2 = exchange(tiles[0], tiles[2], 4)
    t1, t3 = exchange(tiles[1], tiles[3], 4)
    return (*exchange(t0, t1, 2), *exchange(t2, t3, 2))


def to_rows(tiles):
    count = tiles.shape[0]
    fours = tiles.reshape(count // 4, 4, ROWS, LANES)
    blocks = transpose_quads([fours[:, i] for i in range(4)])
    return jnp.concatenate(blocks, axis=-1).reshape(count * 2, M)


def to_tiles(rows):
    stacked = rows.reshape(rows.shape[0] // ROWS, ROWS, M)
    blocks = [stacked[:, :, q * LANES : (q + 1) * LANES] for q in range(QUADS)]
    fours = transpose_quads(blocks)
    return [fours[body % 4][body // 4] for body in range(rows.shape[0] // 2)]


def kernel(*refs):
    refs = list(refs)

    def take(count):
        taken = refs[:count]
        del refs[:count]
        return taken

    incident_h, diffraction_h, mixing_h, coupling_h, lists_h, groups_h, jacket_h = take(7)
    coef_out, resp_out = take(2)
    incident, diffraction_v, mixing_v, coupling_v, jacket_v, lists, groups = take(7)
    d_hi, d_lo, m_hi, m_lo, j_hi, j_lo = take(6)
    factor, incoming, own = take(3)
    lists_all, picks, places, named_by, member, picks_s, places_s = take(7)
    sending, shares, aside_parts, totals = take(4)
    pools = [take(TEAMS) for _ in range(ITERS)]
    near = [[take(2) for _ in range(TEAMS)] for _ in range(ITERS)]
    far = [[take(2) for _ in range(TEAMS)] for _ in range(ITERS)]
    in_sems, list_sems, dense_send, near_recv, far_recv, row_send, row_recv, part_sems, share_sems, table_sem = take(10)

    me = lax.axis_index("site")
    z, x = me // NX, me % NX

    z_parts = [(z + dz) % NZ * NX for dz in range(NZ)]
    x_parts = [(x + dx) % NX for dx in range(NX)]

    def at(dz, dx):
        return z_parts[dz % NZ] + x_parts[dx % NX]

    def send(src, dst, send_sem, recv_sem, site):
        pltpu.make_async_remote_copy(
            src_ref=src,
            dst_ref=dst,
            send_sem=send_sem,
            recv_sem=recv_sem,
            device_id={"site": site},
            device_id_type=MESH,
        ).start()

    def done(ref, sem):
        pltpu.make_async_copy(ref, ref, sem).wait()

    def place_of(behind, aside):
        return aside * NZ + (behind + 2) % NZ

    def outgoing_of(sweep, team, tiles):
        coef = product(to_rows(tiles), d_hi, d_lo)
        for body, tile in enumerate(to_tiles(product(coef, m_hi, m_lo))):
            own[sweep, team, body] = tile

    def send_dense(sweep, team):
        for way, step in enumerate(WAYS):
            send(
                own.at[sweep, team],
                near[sweep][team][way],
                dense_send.at[sweep, team],
                near_recv.at[sweep, team, way],
                at(step, 0),
            )

    def pick(sweep, team, block, dz, dx, behind, lane, number, skip):
        row = 2 * place_of((behind + NZ) % NZ, dx) + skip
        entry = ((dz + NZ) % NZ) * NX + dx
        for i in range(number):
            sending[sweep, team, row + i] = block[picks_s[entry, lane + skip + i]]
        return row

    def send_rows(sweep, team, row, number, dz, dx):
        send(
            sending.at[sweep, team, pl.ds(row, number)],
            pools[sweep][team].at[pl.ds(row, number)],
            row_send.at[sweep, team],
            row_recv.at[sweep, team],
            at(dz, dx),
        )

    def pick_aside(sweep, team):
        for dx in range(1, NX):
            pick(sweep, team, own.at[sweep, team], 0, dx, 0, 0, 2, 0)

    def pass_near(sweep, team):
        for way, step in enumerate(WAYS):
            done(near[sweep][team][way], near_recv.at[sweep, team, way])
            send(
                near[sweep][team][way],
                far[sweep][team][way],
                dense_send.at[sweep, team],
                far_recv.at[sweep, team, way],
                at(step, 0),
            )

    def pick_near(sweep, team):
        for dx in range(1, NX):
            for way, step in enumerate(WAYS):
                pick(sweep, team, near[sweep][team][way], 0, dx, step, 2 + 2 * way, 2, 0)
            send_rows(sweep, team, 2 * place_of(NZ - 1, dx), 6, 0, dx)

    def pass_far(sweep, team):
        for way in range(2):
            done(far[sweep][team][way], far_recv.at[sweep, team, way])

        for hop, number in ((2, 1), (0, 2), (1, 2)):
            for dx in range(NX):
                for way, step in enumerate(WAYS):
                    if hop > 0 or dx > 0:
                        skip = way if hop == 2 else 0
                        row = pick(
                            sweep,
                            team,
                            far[sweep][team][way],
                            step * hop,
                            dx,
                            step * (hop + 2),
                            6 + 2 * way,
                            number,
                            skip,
                        )
                        send_rows(sweep, team, row, number, step * hop, dx)

        pool = pools[sweep][team]
        pool[2 * SITES :] = own[sweep, team]
        for way, step in enumerate(WAYS):
            for distance, blocks in ((1, near), (2, far)):
                row = 2 * place_of((step * distance + NZ) % NZ, 0)
                for i in range(2):
                    pool[row + i] = blocks[sweep][team][way][picks_s[0, 4 * distance - 2 + 2 * way + i]]

    def gather(sweep, team):
        pool = pools[sweep][team]
        done(pool.at[pl.ds(LOCAL, 2 * SITES - LOCAL)], row_recv.at[sweep, team])

        @pl.loop(0, BDEV // 4)
        def _(four):
            for i in range(4):
                body = 4 * four + i
                straight = incident[body, team]
                turned = jnp.zeros((ROWS, LANES), F32)
                for k in range(K):
                    value = pool[places_s[k, body]]
                    straight = straight + factor[body, 2 * k] * value
                    turned = turned + factor[body, 2 * k + 1] * value
                incoming[team, body] = straight + turn(turned)

    def share_parts(team):
        bodies = [incoming[team, body] for body in range(BDEV)]

        @pl.loop(0, SITES // 8)
        def _(eight):
            for i in range(8):
                item = eight * 8 + i
                share = member[item, 0:1, :] * bodies[0]
                for body in range(1, BDEV):
                    share = share + member[item, body : body + 1, :] * bodies[body]
                shares[team, item] = share

        if team == TEAMS - 1:
            for dz in (4, 3, 5, 2, 6, 1, 7, 0):
                for dx in range(NX):
                    item = dx * NZ + dz
                    if item > 0:
                        send(
                            shares.at[team, item],
                            aside_parts.at[team, item],
                            part_sems.at[0, team],
                            part_sems.at[1, team],
                            at(dz, dx),
                        )
            return
        for dx in range(1, NX):
            send(
                shares.at[team, pl.ds(dx * NZ, NZ)],
                aside_parts.at[team, pl.ds(dx * NZ, NZ)],
                part_sems.at[0, team],
                part_sems.at[1, team],
                at(0, dx),
            )

    def share_totals(team):
        done(aside_parts.at[team, pl.ds(NZ, SITES - NZ)], part_sems.at[1, team])
        total = shares[team, pl.ds(0, NZ)]
        for dx in range(1, NX):
            total = total + aside_parts[team, pl.ds(dx * NZ, NZ)]
        totals[team, 0] = total
        for dz in range(1, NZ):
            send(
                totals.at[team, 0, dz],
                totals.at[team, 1, dz],
                share_sems.at[0, team],
                share_sems.at[1, team],
                at(dz, 0),
            )

    def store_coefficients(team):
        rows = product(to_rows(incoming[team]), d_hi, d_lo)
        for body, tile in enumerate(to_tiles(rows)):
            coef_out[body, team] = tile

    barrier = pltpu.get_barrier_semaphore()

    for step in range(1, SITES):
        site = at(step // NX, step % NX)
        pl.semaphore_signal(barrier, inc=1, device_id={"site": site}, device_id_type=MESH)

    loads = [
        pltpu.make_async_copy(src, dst, in_sems.at[i])
        for i, (src, dst) in enumerate(
            (
                (incident_h, incident),
                (diffraction_h, diffraction_v),
                (mixing_h, mixing_v),
                (coupling_h, coupling_v),
                (jacket_h, jacket_v),
                (lists_h, lists),
                (groups_h, groups),
            )
        )
    ]
    for load in loads:
        load.start()

    loads[1].wait()
    load_matrix(diffraction_v, d_hi, d_lo)
    loads[2].wait()
    load_matrix(mixing_v, m_hi, m_lo)
    loads[0].wait()
    for team in range(TEAMS):
        outgoing_of(0, team, incident[:, team])

    loads[5].wait()
    own_list = lists[...]
    owner = own_list // BDEV
    local = own_list % BDEV
    sites = lax.broadcasted_iota(jnp.int32, (SITES, K, BDEV), 0)
    named = owner[None] == sites
    last = jnp.where(named, local[None], -1)
    last = jnp.max(jnp.max(last, axis=1, keepdims=True), axis=2, keepdims=True)
    later = jnp.max(jnp.where(named & (local[None] == last), 1, 0), axis=0)
    behind = (z - owner // NX + NZ) % NZ
    aside = (x - owner % NX + NX) % NX
    places[...] = jnp.zeros((K, 128), jnp.int32)
    places[:, :BDEV] = jnp.where(owner == me, 2 * SITES + local, 2 * place_of(behind, aside) + later)
    move_places = pltpu.make_async_copy(places, places_s, table_sem.at[0])
    move_places.start()
    lists_all[0] = own_list

    loads[3].wait()
    real = is_real((ROWS, LANES))

    @pl.loop(0, BDEV)
    def _(body):
        for k in range(K):
            both = coupling_v[body, k]
            factor[body, 2 * k] = jnp.where(real, both, pltpu.roll(both, 1, 0))
            factor[body, 2 * k + 1] = jnp.where(real, pltpu.roll(both, ROWS - 1, 0), both)

    loads[4].wait()
    load_matrix(jacket_v, j_hi, j_lo)
    halves = []
    for part in range(2):
        columns = pl.ds(part * M, M)
        both = jnp.dot(d_hi[:, columns], j_hi[...], preferred_element_type=F32)
        both = both + jnp.dot(d_lo[:, columns], j_hi[...], preferred_element_type=F32)
        halves.append(both + jnp.dot(d_hi[:, columns], j_lo[...], preferred_element_type=F32))
    joint_real = halves[0][:, :NF] - halves[1][:, NF:]
    joint_imag = halves[0][:, NF:] + halves[1][:, :NF]
    j_hi[:, :NF], j_lo[:, :NF] = split(joint_real)
    j_hi[:, NF:], j_lo[:, NF:] = split(joint_imag)

    loads[6].wait()
    for body in range(BDEV):
        named_by[body : body + 1, :] = jnp.full((1, LANES), groups[0, body], jnp.int32)

    for item in range(SITES):
        member[item] = jnp.where(named_by[...] == at(item % NZ, item // NZ), 1.0, 0.0)

    pl.semaphore_wait(barrier, SITES - 1)

    send_dense(0, 0)
    for step in range(1, SITES):
        dz, dx = step // NX, step % NX
        send(
            lists,
            lists_all.at[((NZ - dz) % NZ) * NX + (NX - dx) % NX],
            list_sems.at[0],
            list_sems.at[1],
            at(dz, dx),
        )

    for team in range(1, TEAMS):
        send_dense(0, team)

    done(lists_all.at[1:], list_sems.at[1])
    everyone = lists_all[...]
    lane = lax.broadcasted_iota(jnp.int32, (SITES, 128), 1)
    table = jnp.zeros((SITES, 128), jnp.int32)
    for i, dz in enumerate((0, -1, 1, -2, 2)):
        theirs = everyone // BDEV == at(dz, 0)
        wanted = everyone % BDEV
        smallest = jnp.min(jnp.where(theirs, wanted, BDEV - 1), axis=1)
        largest = jnp.max(jnp.where(theirs, wanted, 0), axis=1)
        table = jnp.where(lane == 2 * i, jnp.min(smallest, axis=1, keepdims=True), table)
        table = jnp.where(lane == 2 * i + 1, jnp.max(largest, axis=1, keepdims=True), table)
    picks[...] = table
    move_picks = pltpu.make_async_copy(picks, picks_s, table_sem.at[1])
    move_picks.start()
    move_places.wait()
    move_picks.wait()

    for sweep in range(ITERS):
        if sweep == 0:
            for team in range(TEAMS):
                pick_aside(sweep, team)
        for team in range(TEAMS):
            pass_near(sweep, team)
            pick_near(sweep, team)
        for team in range(TEAMS):
            pass_far(sweep, team)
        if sweep < ITERS - 1:
            for team in range(TEAMS):
                gather(sweep, team)
                outgoing_of(sweep + 1, team, incoming[team])
                send_dense(sweep + 1, team)
                pick_aside(sweep + 1, team)

    for team in range(TEAMS):
        gather(ITERS - 1, team)
        share_parts(team)
        if team > 0:
            share_totals(team - 1)
        store_coefficients(team)

    done(lists_all.at[1:], list_sems.at[0])
    for sweep in range(ITERS):
        for team in range(TEAMS):
            done(own.at[sweep], dense_send.at[sweep, team])
            done(sending.at[sweep, team, pl.ds(LOCAL, 2 * SITES - LOCAL)], row_send.at[sweep, team])

    def done_sums():
        for team in range(TEAMS):
            if team == TEAMS - 1:
                done(shares.at[team, pl.ds(1, SITES - 1)], part_sems.at[0, team])
                continue
            done(shares.at[team, pl.ds(NZ, SITES - NZ)], part_sems.at[0, team])
            done(totals.at[team, 0, pl.ds(1, NZ - 1)], share_sems.at[0, team])

    sums = []
    for team in range(TEAMS):
        if team == TEAMS - 1:
            done(aside_parts.at[team, pl.ds(1, SITES - 1)], part_sems.at[1, team])
            parts = [shares[team, 0]] + [aside_parts[team, item] for item in range(1, SITES)]
            while len(parts) > 1:
                parts = [a + b for a, b in zip(parts[::2], parts[1::2])]
            sums.append(parts[0][None])
            continue
        done(totals.at[team, 1, pl.ds(1, NZ - 1)], share_sems.at[1, team])
        total = totals[team, 0, 0]
        for dz in range(1, NZ):
            total = total + totals[team, 1, dz]
        sums.append(total[None])
    total = jnp.concatenate(transpose_quads(sums), axis=-1)[0]
    resp_out[...] = product(total, j_hi, j_lo)
    done_sums()


def to_native(values):
    lead = values.shape[:-2]
    return jnp.swapaxes(values.reshape(*lead, 2, QUADS, LANES), -3, -2).reshape(*lead, ROWS, LANES)


def from_native(tiles):
    lead = tiles.shape[:-2]
    return jnp.swapaxes(tiles.reshape(*lead, QUADS, 2, LANES), -3, -2).reshape(*lead, 2, M)


def per_device(incident, diffraction, mixing, coupling, lists, groups, jacket):
    vmem = pl.BlockSpec(memory_space=pltpu.VMEM)
    anywhere = pl.BlockSpec(memory_space=pl.ANY)

    def f32(*shape):
        return pltpu.VMEM(shape, F32)

    def i32(*shape):
        return pltpu.VMEM(shape, jnp.int32)

    def dma(*shape):
        return pltpu.SemaphoreType.DMA(shape)

    coef, resp = pl.pallas_call(
        kernel,
        out_shape=(
            jax.ShapeDtypeStruct((BDEV, TEAMS, ROWS, LANES), F32),
            jax.ShapeDtypeStruct((ROWS, NF), F32),
        ),
        in_specs=[anywhere] * 7,
        out_specs=(vmem, vmem),
        scratch_shapes=[
            f32(BDEV, TEAMS, ROWS, LANES),
            f32(2, M, M),
            f32(2, M, M),
            f32(BDEV, K, ROWS, LANES),
            f32(2, M, NF),
            i32(K, BDEV),
            pltpu.SMEM((1, BDEV), jnp.int32),
            *[pltpu.VMEM((M, 2 * M), BF16)] * 4,
            *[pltpu.VMEM((M, 2 * NF), BF16)] * 2,
            f32(BDEV, 2 * K, ROWS, LANES),
            f32(TEAMS, BDEV, ROWS, LANES),
            f32(ITERS, TEAMS, BDEV, ROWS, LANES),
            i32(SITES, K, BDEV),
            i32(SITES, 128),
            i32(K, 128),
            i32(BDEV, LANES),
            f32(SITES, BDEV, LANES),
            pltpu.SMEM((SITES, 128), jnp.int32),
            pltpu.SMEM((K, 128), jnp.int32),
            f32(ITERS, TEAMS, 2 * SITES, ROWS, LANES),
            f32(TEAMS, SITES, ROWS, LANES),
            f32(TEAMS, SITES, ROWS, LANES),
            f32(TEAMS, 2, NZ, ROWS, LANES),
            *[f32(POOL, ROWS, LANES)] * (ITERS * TEAMS),
            *[f32(BDEV, ROWS, LANES)] * (ITERS * TEAMS * 4),
            dma(7),
            dma(2),
            dma(ITERS, TEAMS),
            dma(ITERS, TEAMS, 2),
            dma(ITERS, TEAMS, 2),
            dma(ITERS, TEAMS),
            dma(ITERS, TEAMS),
            dma(2, TEAMS),
            dma(2, TEAMS),
            dma(2),
        ],
        compiler_params=pltpu.CompilerParams(
            collective_id=0, has_side_effects=True, vmem_limit_bytes=44 * 1024 * 1024
        ),
        cost_estimate=pl.CostEstimate(
            flops=3_000_000_000, bytes_accessed=6_000_000, transcendentals=0
        ),
    )(
        *[
            pltpu.with_memory_space_constraint(operand, pltpu.HBM)
            for operand in (
                to_native(incident),
                diffraction,
                mixing,
                to_native(coupling),
                lists.T,
                groups.reshape(1, BDEV),
                jacket.reshape(2, M, NF),
            )
        ]
    )
    return from_native(coef), resp.reshape(1, 4, 2, NF)


def solution(mesh):
    placed = (
        P("site", "freq", None, None),
        P("freq", None, None),
        P("freq", None, None),
        P("site", "freq", None, None),
        P("site", None),
        P("site", None),
        P("site", "freq", None, None),
    )
    return jax.shard_map(
        per_device,
        mesh=mesh,
        in_specs=placed,
        out_specs=(P("site", "freq", None, None), P("site", "freq", None, None)),
        check_vma=False,
    )
```

```python
import jax
import jax.numpy as jnp
from jax import lax
from jax.experimental import pallas as pl
from jax.experimental.pallas import tpu as pltpu
from jax.sharding import PartitionSpec as P

ITERS = 3
NZ = 8
NX = 4
SITES = NZ * NX
BDEV = 16
K = 8
M = 512
LANES = 128
QUADS = M // LANES
NF = 128
ROWS = 8
TEAMS = 4
POOL = 2 * SITES + BDEV
LOCAL = 10
WAYS = (1, -1)
MESH = pl.DeviceIdType.MESH
F32 = jnp.float32
BF16 = jnp.bfloat16


def split(x):
    hi = x.astype(BF16)
    lo = (x - hi.astype(F32)).astype(BF16)
    return hi, lo


def is_real(shape):
    return lax.broadcasted_iota(jnp.int32, shape, 0) % 2 == 0


def turn(x):
    n = x.shape[0]
    return jnp.where(is_real(x.shape), -pltpu.roll(x, n - 1, 0), pltpu.roll(x, 1, 0))


def product(x, w_hi, w_lo):
    rows, width = x.shape[0], w_hi.shape[1] // 2
    x_hi, x_lo = split(x)
    y = jnp.dot(jnp.concatenate([x_hi, x_lo], axis=0), w_hi[...], preferred_element_type=F32)
    y = y[:rows] + y[rows:] + jnp.dot(x_hi, w_lo[...], preferred_element_type=F32)
    return y[:, :width] + turn(y[:, width:])


def load_matrix(src, w_hi, w_lo):
    width = src.shape[2]
    for part in range(2):
        hi, lo = split(src[part])
        w_hi[:, part * width : (part + 1) * width] = hi
        w_lo[:, part * width : (part + 1) * width] = lo


def exchange(a, b, span):
    even = lax.broadcasted_iota(jnp.int32, a.shape, 1) // span % 2 == 0
    first = jnp.where(even, a, pltpu.roll(b, span, 1))
    second = jnp.where(even, pltpu.roll(a, ROWS - span, 1), b)
    return first, second


def transpose_quads(tiles):
    t0, t2 = exchange(tiles[0], tiles[2], 4)
    t1, t3 = exchange(tiles[1], tiles[3], 4)
    return (*exchange(t0, t1, 2), *exchange(t2, t3, 2))


def to_rows(tiles):
    count = tiles.shape[0]
    fours = tiles.reshape(count // 4, 4, ROWS, LANES)
    blocks = transpose_quads([fours[:, i] for i in range(4)])
    return jnp.concatenate(blocks, axis=-1).reshape(count * 2, M)


def to_tiles(rows):
    stacked = rows.reshape(rows.shape[0] // ROWS, ROWS, M)
    blocks = [stacked[:, :, q * LANES : (q + 1) * LANES] for q in range(QUADS)]
    fours = transpose_quads(blocks)
    return [fours[body % 4][body // 4] for body in range(rows.shape[0] // 2)]


def kernel(*refs):
    refs = list(refs)

    def take(count):
        taken = refs[:count]
        del refs[:count]
        return taken

    incident_h, diffraction_h, mixing_h, coupling_h, lists_h, groups_h, jacket_h = take(7)
    coef_out, resp_out = take(2)
    incident, diffraction_v, mixing_v, coupling_v, jacket_v, lists, groups = take(7)
    d_hi, d_lo, m_hi, m_lo, j_hi, j_lo = take(6)
    factor, incoming, own = take(3)
    lists_all, picks, places, named_by, member, picks_s, places_s = take(7)
    sending, shares, aside_parts, totals = take(4)
    pools = [take(TEAMS) for _ in range(ITERS)]
    near = [[take(2) for _ in range(TEAMS)] for _ in range(ITERS)]
    far = [[take(2) for _ in range(TEAMS)] for _ in range(ITERS)]
    in_sems, list_sems, dense_send, near_recv, far_recv, row_send, row_recv, part_sems, share_sems, table_sem = take(10)

    me = lax.axis_index("site")
    z, x = me // NX, me % NX

    z_parts = [(z + dz) % NZ * NX for dz in range(NZ)]
    x_parts = [(x + dx) % NX for dx in range(NX)]

    def at(dz, dx):
        return z_parts[dz % NZ] + x_parts[dx % NX]

    def send(src, dst, send_sem, recv_sem, site):
        pltpu.make_async_remote_copy(
            src_ref=src,
            dst_ref=dst,
            send_sem=send_sem,
            recv_sem=recv_sem,
            device_id={"site": site},
            device_id_type=MESH,
        ).start()

    def done(ref, sem):
        pltpu.make_async_copy(ref, ref, sem).wait()

    def place_of(behind, aside):
        return aside * NZ + (behind + 2) % NZ

    def outgoing_of(sweep, team, tiles):
        coef = product(to_rows(tiles), d_hi, d_lo)
        for body, tile in enumerate(to_tiles(product(coef, m_hi, m_lo))):
            own[sweep, team, body] = tile

    def send_dense(sweep, team):
        for way, step in enumerate(WAYS):
            send(
                own.at[sweep, team],
                near[sweep][team][way],
                dense_send.at[sweep, team],
                near_recv.at[sweep, team, way],
                at(step, 0),
            )

    def pick(sweep, team, block, dz, dx, behind, lane, number, skip):
        row = 2 * place_of((behind + NZ) % NZ, dx) + skip
        entry = ((dz + NZ) % NZ) * NX + dx
        for i in range(number):
            sending[sweep, team, row + i] = block[picks_s[entry, lane + skip + i]]
        return row

    def send_rows(sweep, team, row, number, dz, dx):
        send(
            sending.at[sweep, team, pl.ds(row, number)],
            pools[sweep][team].at[pl.ds(row, number)],
            row_send.at[sweep, team],
            row_recv.at[sweep, team],
            at(dz, dx),
        )

    def pick_aside(sweep, team):
        for dx in range(1, NX):
            pick(sweep, team, own.at[sweep, team], 0, dx, 0, 0, 2, 0)

    def pass_near(sweep, team):
        for way, step in enumerate(WAYS):
            done(near[sweep][team][way], near_recv.at[sweep, team, way])
            send(
                near[sweep][team][way],
                far[sweep][team][way],
                dense_send.at[sweep, team],
                far_recv.at[sweep, team, way],
                at(step, 0),
            )

    def pick_near(sweep, team):
        for dx in range(1, NX):
            for way, step in enumerate(WAYS):
                pick(sweep, team, near[sweep][team][way], 0, dx, step, 2 + 2 * way, 2, 0)
            send_rows(sweep, team, 2 * place_of(NZ - 1, dx), 6, 0, dx)

    def pass_far(sweep, team):
        for way in range(2):
            done(far[sweep][team][way], far_recv.at[sweep, team, way])

        for hop, number in ((2, 1), (0, 2), (1, 2)):
            for dx in range(NX):
                for way, step in enumerate(WAYS):
                    if hop > 0 or dx > 0:
                        skip = way if hop == 2 else 0
                        row = pick(
                            sweep,
                            team,
                            far[sweep][team][way],
                            step * hop,
                            dx,
                            step * (hop + 2),
                            6 + 2 * way,
                            number,
                            skip,
                        )
                        send_rows(sweep, team, row, number, step * hop, dx)

        pool = pools[sweep][team]
        pool[2 * SITES :] = own[sweep, team]
        for way, step in enumerate(WAYS):
            for distance, blocks in ((1, near), (2, far)):
                row = 2 * place_of((step * distance + NZ) % NZ, 0)
                for i in range(2):
                    pool[row + i] = blocks[sweep][team][way][picks_s[0, 4 * distance - 2 + 2 * way + i]]

    def gather(sweep, team):
        pool = pools[sweep][team]
        done(pool.at[pl.ds(LOCAL, 2 * SITES - LOCAL)], row_recv.at[sweep, team])

        @pl.loop(0, BDEV // 4)
        def _(four):
            for i in range(4):
                body = 4 * four + i
                straight = incident[body, team]
                turned = jnp.zeros((ROWS, LANES), F32)
                for k in range(K):
                    value = pool[places_s[k, body]]
                    straight = straight + factor[body, 2 * k] * value
                    turned = turned + factor[body, 2 * k + 1] * value
                incoming[team, body] = straight + turn(turned)

    def share_parts(team):
        bodies = [incoming[team, body] for body in range(BDEV)]

        @pl.loop(0, SITES // 8)
        def _(eight):
            for i in range(8):
                item = eight * 8 + i
                share = member[item, 0:1, :] * bodies[0]
                for body in range(1, BDEV):
                    share = share + member[item, body : body + 1, :] * bodies[body]
                shares[team, item] = share

        if team == TEAMS - 1:
            for dz in (4, 3, 5, 2, 6, 1, 7, 0):
                for dx in range(NX):
                    item = dx * NZ + dz
                    if item > 0:
                        send(
                            shares.at[team, item],
                            aside_parts.at[team, item],
                            part_sems.at[0, team],
                            part_sems.at[1, team],
                            at(dz, dx),
                        )
            return
        for dx in range(1, NX):
            send(
                shares.at[team, pl.ds(dx * NZ, NZ)],
                aside_parts.at[team, pl.ds(dx * NZ, NZ)],
                part_sems.at[0, team],
                part_sems.at[1, team],
                at(0, dx),
            )

    def share_totals(team):
        done(aside_parts.at[team, pl.ds(NZ, SITES - NZ)], part_sems.at[1, team])
        total = shares[team, pl.ds(0, NZ)]
        for dx in range(1, NX):
            total = total + aside_parts[team, pl.ds(dx * NZ, NZ)]
        totals[team, 0] = total
        for dz in range(1, NZ):
            send(
                totals.at[team, 0, dz],
                totals.at[team, 1, dz],
                share_sems.at[0, team],
                share_sems.at[1, team],
                at(dz, 0),
            )

    def store_coefficients(team):
        rows = product(to_rows(incoming[team]), d_hi, d_lo)
        for body, tile in enumerate(to_tiles(rows)):
            coef_out[body, team] = tile

    barrier = pltpu.get_barrier_semaphore()

    for step in range(1, SITES):
        site = at(step // NX, step % NX)
        pl.semaphore_signal(barrier, inc=1, device_id={"site": site}, device_id_type=MESH)

    loads = [
        pltpu.make_async_copy(src, dst, in_sems.at[i])
        for i, (src, dst) in enumerate(
            (
                (incident_h, incident),
                (diffraction_h, diffraction_v),
                (mixing_h, mixing_v),
                (coupling_h, coupling_v),
                (jacket_h, jacket_v),
                (lists_h, lists),
                (groups_h, groups),
            )
        )
    ]
    for load in loads:
        load.start()

    loads[1].wait()
    load_matrix(diffraction_v, d_hi, d_lo)
    loads[2].wait()
    load_matrix(mixing_v, m_hi, m_lo)
    loads[0].wait()
    for team in range(TEAMS):
        outgoing_of(0, team, incident[:, team])

    loads[5].wait()
    own_list = lists[...]
    owner = own_list // BDEV
    local = own_list % BDEV
    sites = lax.broadcasted_iota(jnp.int32, (SITES, K, BDEV), 0)
    named = owner[None] == sites
    last = jnp.where(named, local[None], -1)
    last = jnp.max(jnp.max(last, axis=1, keepdims=True), axis=2, keepdims=True)
    later = jnp.max(jnp.where(named & (local[None] == last), 1, 0), axis=0)
    behind = (z - owner // NX + NZ) % NZ
    aside = (x - owner % NX + NX) % NX
    places[...] = jnp.zeros((K, 128), jnp.int32)
    places[:, :BDEV] = jnp.where(owner == me, 2 * SITES + local, 2 * place_of(behind, aside) + later)
    move_places = pltpu.make_async_copy(places, places_s, table_sem.at[0])
    move_places.start()
    lists_all[0] = own_list

    loads[3].wait()
    real = is_real((ROWS, LANES))

    @pl.loop(0, BDEV)
    def _(body):
        for k in range(K):
            both = coupling_v[body, k]
            factor[body, 2 * k] = jnp.where(real, both, pltpu.roll(both, 1, 0))
            factor[body, 2 * k + 1] = jnp.where(real, pltpu.roll(both, ROWS - 1, 0), both)

    loads[4].wait()
    load_matrix(jacket_v, j_hi, j_lo)
    halves = []
    for part in range(2):
        columns = pl.ds(part * M, M)
        both = jnp.dot(d_hi[:, columns], j_hi[...], preferred_element_type=F32)
        both = both + jnp.dot(d_lo[:, columns], j_hi[...], preferred_element_type=F32)
        halves.append(both + jnp.dot(d_hi[:, columns], j_lo[...], preferred_element_type=F32))
    joint_real = halves[0][:, :NF] - halves[1][:, NF:]
    joint_imag = halves[0][:, NF:] + halves[1][:, :NF]
    j_hi[:, :NF], j_lo[:, :NF] = split(joint_real)
    j_hi[:, NF:], j_lo[:, NF:] = split(joint_imag)

    loads[6].wait()
    for body in range(BDEV):
        named_by[body : body + 1, :] = jnp.full((1, LANES), groups[0, body], jnp.int32)

    for item in range(SITES):
        member[item] = jnp.where(named_by[...] == at(item % NZ, item // NZ), 1.0, 0.0)

    pl.semaphore_wait(barrier, SITES - 1)

    send_dense(0, 0)
    for step in range(1, SITES):
        dz, dx = step // NX, step % NX
        send(
            lists,
            lists_all.at[((NZ - dz) % NZ) * NX + (NX - dx) % NX],
            list_sems.at[0],
            list_sems.at[1],
            at(dz, dx),
        )

    for team in range(1, TEAMS):
        send_dense(0, team)

    done(lists_all.at[1:], list_sems.at[1])
    everyone = lists_all[...]
    lane = lax.broadcasted_iota(jnp.int32, (SITES, 128), 1)
    table = jnp.zeros((SITES, 128), jnp.int32)
    for i, dz in enumerate((0, -1, 1, -2, 2)):
        theirs = everyone // BDEV == at(dz, 0)
        wanted = everyone % BDEV
        smallest = jnp.min(jnp.where(theirs, wanted, BDEV - 1), axis=1)
        largest = jnp.max(jnp.where(theirs, wanted, 0), axis=1)
        table = jnp.where(lane == 2 * i, jnp.min(smallest, axis=1, keepdims=True), table)
        table = jnp.where(lane == 2 * i + 1, jnp.max(largest, axis=1, keepdims=True), table)
    picks[...] = table
    move_picks = pltpu.make_async_copy(picks, picks_s, table_sem.at[1])
    move_picks.start()
    move_places.wait()
    move_picks.wait()

    for sweep in range(ITERS):
        for team in range(TEAMS):
            pass_near(sweep, team)
            pick_aside(sweep, team)
            pick_near(sweep, team)
        for team in range(TEAMS):
            pass_far(sweep, team)
        if sweep < ITERS - 1:
            for team in range(TEAMS):
                gather(sweep, team)
                outgoing_of(sweep + 1, team, incoming[team])
                send_dense(sweep + 1, team)

    for team in range(TEAMS):
        gather(ITERS - 1, team)
        share_parts(team)
        if team > 0:
            share_totals(team - 1)
        store_coefficients(team)

    done(lists_all.at[1:], list_sems.at[0])
    for sweep in range(ITERS):
        for team in range(TEAMS):
            done(own.at[sweep], dense_send.at[sweep, team])
            done(sending.at[sweep, team, pl.ds(LOCAL, 2 * SITES - LOCAL)], row_send.at[sweep, team])

    def done_sums():
        for team in range(TEAMS):
            if team == TEAMS - 1:
                done(shares.at[team, pl.ds(1, SITES - 1)], part_sems.at[0, team])
                continue
            done(shares.at[team, pl.ds(NZ, SITES - NZ)], part_sems.at[0, team])
            done(totals.at[team, 0, pl.ds(1, NZ - 1)], share_sems.at[0, team])

    sums = []
    for team in range(TEAMS):
        if team == TEAMS - 1:
            done(aside_parts.at[team, pl.ds(1, SITES - 1)], part_sems.at[1, team])
            parts = [shares[team, 0]] + [aside_parts[team, item] for item in range(1, SITES)]
            while len(parts) > 1:
                parts = [a + b for a, b in zip(parts[::2], parts[1::2])]
            sums.append(parts[0][None])
            continue
        done(totals.at[team, 1, pl.ds(1, NZ - 1)], share_sems.at[1, team])
        total = totals[team, 0, 0]
        for dz in range(1, NZ):
            total = total + totals[team, 1, dz]
        sums.append(total[None])
    total = jnp.concatenate(transpose_quads(sums), axis=-1)[0]
    resp_out[...] = product(total, j_hi, j_lo)
    done_sums()


def to_native(values):
    lead = values.shape[:-2]
    return jnp.swapaxes(values.reshape(*lead, 2, QUADS, LANES), -3, -2).reshape(*lead, ROWS, LANES)


def from_native(tiles):
    lead = tiles.shape[:-2]
    return jnp.swapaxes(tiles.reshape(*lead, QUADS, 2, LANES), -3, -2).reshape(*lead, 2, M)


def per_device(incident, diffraction, mixing, coupling, lists, groups, jacket):
    vmem = pl.BlockSpec(memory_space=pltpu.VMEM)
    anywhere = pl.BlockSpec(memory_space=pl.ANY)

    def f32(*shape):
        return pltpu.VMEM(shape, F32)

    def i32(*shape):
        return pltpu.VMEM(shape, jnp.int32)

    def dma(*shape):
        return pltpu.SemaphoreType.DMA(shape)

    coef, resp = pl.pallas_call(
        kernel,
        out_shape=(
            jax.ShapeDtypeStruct((BDEV, TEAMS, ROWS, LANES), F32),
            jax.ShapeDtypeStruct((ROWS, NF), F32),
        ),
        in_specs=[anywhere] * 7,
        out_specs=(vmem, vmem),
        scratch_shapes=[
            f32(BDEV, TEAMS, ROWS, LANES),
            f32(2, M, M),
            f32(2, M, M),
            f32(BDEV, K, ROWS, LANES),
            f32(2, M, NF),
            i32(K, BDEV),
            pltpu.SMEM((1, BDEV), jnp.int32),
            *[pltpu.VMEM((M, 2 * M), BF16)] * 4,
            *[pltpu.VMEM((M, 2 * NF), BF16)] * 2,
            f32(BDEV, 2 * K, ROWS, LANES),
            f32(TEAMS, BDEV, ROWS, LANES),
            f32(ITERS, TEAMS, BDEV, ROWS, LANES),
            i32(SITES, K, BDEV),
            i32(SITES, 128),
            i32(K, 128),
            i32(BDEV, LANES),
            f32(SITES, BDEV, LANES),
            pltpu.SMEM((SITES, 128), jnp.int32),
            pltpu.SMEM((K, 128), jnp.int32),
            f32(ITERS, TEAMS, 2 * SITES, ROWS, LANES),
            f32(TEAMS, SITES, ROWS, LANES),
            f32(TEAMS, SITES, ROWS, LANES),
            f32(TEAMS, 2, NZ, ROWS, LANES),
            *[f32(POOL, ROWS, LANES)] * (ITERS * TEAMS),
            *[f32(BDEV, ROWS, LANES)] * (ITERS * TEAMS * 4),
            dma(7),
            dma(2),
            dma(ITERS, TEAMS),
            dma(ITERS, TEAMS, 2),
            dma(ITERS, TEAMS, 2),
            dma(ITERS, TEAMS),
            dma(ITERS, TEAMS),
            dma(2, TEAMS),
            dma(2, TEAMS),
            dma(2),
        ],
        compiler_params=pltpu.CompilerParams(
            collective_id=0, has_side_effects=True, vmem_limit_bytes=44 * 1024 * 1024
        ),
        cost_estimate=pl.CostEstimate(
            flops=3_000_000_000, bytes_accessed=6_000_000, transcendentals=0
        ),
    )(
        *[
            pltpu.with_memory_space_constraint(operand, pltpu.HBM)
            for operand in (
                to_native(incident),
                diffraction,
                mixing,
                to_native(coupling),
                lists.T,
                groups.reshape(1, BDEV),
                jacket.reshape(2, M, NF),
            )
        ]
    )
    return from_native(coef), resp.reshape(1, 4, 2, NF)


def solution(mesh):
    placed = (
        P("site", "freq", None, None),
        P("freq", None, None),
        P("freq", None, None),
        P("site", "freq", None, None),
        P("site", None),
        P("site", None),
        P("site", "freq", None, None),
    )
    return jax.shard_map(
        per_device,
        mesh=mesh,
        in_specs=placed,
        out_specs=(P("site", "freq", None, None), P("site", "freq", None, None)),
        check_vma=False,
    )
```
